512 devices in a mesh: space: 32 (over y, z_lo, core), date: 16 (over x, z_hi).
Axes of the slice: x: 4, y: 4, z: 16 (z_hi: 4, z_lo: 4; z = z_hi * 4 + z_lo), core: 2. Of those that a mesh axis runs over, the one named last changes fastest.
Arguments:
- hr_qkv: bfloat16 [3, 16, 256, 16, 2816], P(None, 'date', 'space'), may hold values from -70 to 70
- s_qkv: bfloat16 [3, 16, 256, 16, 1024], P(None, 'date', 'space'), may hold values from -70 to 70
- hr_proj: bfloat16 [2816, 2816], P(None, 'date'), may hold values from -0.109375 to 0.109375
- s_proj: bfloat16 [1024, 1024], P('date'), may hold values from -0.1875 to 0.1875
- shifts: int32 [16], P('date'), may hold values from 0 to 4
- cloud_valid: int32 [16, 256, 16], P(None, 'space', 'date'), may hold values 0 or 1
- date_embed: bfloat16 [16, 3840], replicated, may hold values from -16 to 16
- norm_gain: float32 [3840], replicated, may hold values from 0.1 to 1.9
Outputs:
- merged_out: bfloat16 [16, 256, 16, 3840], P(None, 'space', 'date')
The draws below stay inside these ranges and needn't reach their ends.
All inputs are finite; a program needn't handle non-finite values. No bound on the sum of `cloud_valid` on one device may be relied on, other than what follows from the above.
Results may differ from the reference program's by a relative error of at most 0.008.
Values may be sent and summed in bfloat16 or wider, within the bound.
No kernel may reach another device: no remote copies, remote signals or barrier semaphores. Data moves between devices by JAX's collectives and lax.ppermute only.
A program may use at most 128 MiB of HBM per device.

```python
import jax
import jax.numpy as jnp
from jax import lax

HRW = 2816
SW = 1024
HR_HEAD = 32
S_HEAD = 64
T_HEAD = 64
WIN = 8
ROW_DEV = 8
COLS = 16
DATES = 16
NROWS = 256
F = 3840


def draw_hr_qkv(key, part):
    key = jax.random.fold_in(key, 11)
    shape = (3, DATES, NROWS, COLS, HRW)
    base = jnp.clip(jax.random.normal(key, shape, jnp.float32), -6.0, 6.0)
    return base.astype(jnp.bfloat16)


def draw_s_qkv(key, part):
    key = jax.random.fold_in(key, 23)
    shape = (3, DATES, NROWS, COLS, SW)
    base = jnp.clip(jax.random.normal(key, shape, jnp.float32), -6.0, 6.0)
    return base.astype(jnp.bfloat16)


def draw_date_embed(key, part):
    key = jax.random.fold_in(key, 37)
    first = jax.random.fold_in(key, 0)
    base = jnp.clip(jax.random.normal(first, (DATES, HRW + SW), jnp.float32), -4.0, 4.0)
    return base.astype(jnp.bfloat16)


def with_ends(drawn, stream_key, smallest, largest):
    place = [jax.random.randint(jax.random.fold_in(stream_key, axis), (), 0, length) for axis, length in enumerate(drawn.shape)]
    widest = drawn.shape.index(max(drawn.shape))
    next_to = place[:widest] + [(place[widest] + 1) % drawn.shape[widest]] + place[widest + 1:]
    return drawn.at[tuple(place)].set(smallest).at[tuple(next_to)].set(largest)


def block_levels(rng, extent, pieces, least, largest):
    def one(dim, blocks):
        steps = jax.random.uniform(jax.random.fold_in(jax.random.fold_in(rng, 6), dim), (blocks,), jnp.float32, least / len(pieces), largest / len(pieces))
        return jnp.repeat(jnp.exp(steps), extent[dim] // blocks).reshape((-1,) + (1,) * (len(extent) - dim - 1))

    factor_of = one(*pieces[0])
    for cut in pieces[1:]:
        factor_of = factor_of * one(*cut)
    return factor_of


def noise(own_key, extent, deviation, bound, shards=(), kind=jnp.bfloat16):
    loudness = block_levels(own_key, extent, shards, -0.22, 0.18) if shards else 1.0
    drawn = jax.random.normal(own_key, extent, jnp.float32) * deviation * loudness
    return jnp.minimum(jnp.maximum(drawn, -bound), bound).astype(kind)


def setup_inputs(seed: int = 0) -> dict:
    streams_of = jax.random.split(jax.random.key(seed), 9)
    return {
        "hr_qkv": draw_hr_qkv(jax.random.fold_in(streams_of[8], 71), 0),
        "s_qkv": draw_s_qkv(jax.random.fold_in(streams_of[8], 71), 0),
        "hr_proj": noise(streams_of[2], (HRW, HRW), HRW ** -0.5, 0.109375, ((1, 16),)),
        "s_proj": noise(streams_of[3], (SW, SW), SW ** -0.5, 0.1875, ((0, 16),)),
        "shifts": with_ends(jax.random.randint(streams_of[4], (DATES,), 0, WIN // 2 + 1), jax.random.fold_in(streams_of[4], 1), 0, (WIN // 2 + 1) - 1).astype(jnp.int32),
        "cloud_valid": with_ends((jax.random.randint(streams_of[5], (DATES, NROWS, COLS), 0, 4) < 3).astype(jnp.int32), jax.random.fold_in(streams_of[5], 1), 0, 1),
        "date_embed": draw_date_embed(jax.random.fold_in(streams_of[8], 71), 0),
        "norm_gain": jnp.clip(1.0 + 0.18 * jax.random.normal(streams_of[7], (F,), jnp.float32), 0.1, 1.9),
    }


def attend(queries, key_part, value_part, head_dim):
    scores = jnp.einsum('nqhd,nkhd->nhqk', queries.astype(jnp.float32), key_part.astype(jnp.float32))
    scores = scores * (1.0 / head_dim ** 0.5)
    scores = scores - lax.optimization_barrier(jnp.max(scores, axis=-1, keepdims=True))
    expo = jnp.exp(scores)
    weights = (expo / lax.optimization_barrier(jnp.sum(expo, axis=-1, keepdims=True))).astype(jnp.bfloat16)
    mixed = jnp.einsum('nhqk,nkhd->nqhd', weights.astype(jnp.float32), value_part.astype(jnp.float32))
    return mixed.astype(jnp.bfloat16).reshape(mixed.shape[0], mixed.shape[1], -1)

def window_attention(queries, key_part, value_part, head_dim):
    row_count, col_count, width = queries.shape

    def split(tensor):
        tensor = tensor.reshape(row_count // WIN, WIN, col_count // WIN, WIN, width // head_dim, head_dim)
        return tensor.transpose(0, 2, 1, 3, 4, 5).reshape(-1, WIN * WIN, width // head_dim, head_dim)
    mixed = attend(split(queries), split(key_part), split(value_part), head_dim)
    mixed = mixed.reshape(row_count // WIN, col_count // WIN, WIN, WIN, width).transpose(0, 2, 1, 3, 4)
    return mixed.reshape(row_count, col_count, width)

def temporal(merged, valid, date_embed, norm_gain):
    date_count, patch_count, channels = merged.shape
    joined = (merged.astype(jnp.float32) + date_embed.astype(jnp.float32)[:, None, :]).astype(jnp.bfloat16)
    heads = joined.reshape(date_count, patch_count, channels // T_HEAD, T_HEAD).astype(jnp.float32)
    scores = jnp.einsum('tphd,sphd->phts', heads, heads) * (1.0 / T_HEAD)
    same = lax.broadcasted_iota(jnp.int32, (date_count, date_count), 0) == lax.broadcasted_iota(jnp.int32, (date_count, date_count), 1)
    keep = (valid.T[:, None, None, :] > 0) | same[None, None]
    scores = jnp.where(keep, scores, jnp.float32(-1e+30))
    scores = scores - lax.optimization_barrier(jnp.max(scores, axis=-1, keepdims=True))
    expo = jnp.where(keep, jnp.exp(scores), jnp.float32(0.0))
    weights = (expo / lax.optimization_barrier(jnp.sum(expo, axis=-1, keepdims=True))).astype(jnp.bfloat16)
    mixed_heads = jnp.einsum('phts,sphd->tphd', weights.astype(jnp.float32), heads)
    mixed = joined.astype(jnp.float32) + mixed_heads.reshape(date_count, patch_count, channels)
    scale = lax.rsqrt(lax.optimization_barrier(jnp.mean(mixed * mixed, axis=-1, keepdims=True)) + 1e-06)
    return (mixed * scale * norm_gain).astype(jnp.bfloat16)

def reference(hr_qkv, s_qkv, hr_proj, s_proj, shifts, cloud_valid, date_embed, norm_gain):

    def one_date(items):
        hr_one, s_one, offset = items
        shifted = jnp.roll(jnp.roll(hr_one, -offset, axis=1), -offset, axis=2)
        mixed = window_attention(shifted[0], shifted[1], shifted[2], HR_HEAD)
        mixed = jnp.roll(jnp.roll(mixed, offset, axis=0), offset, axis=1)
        hr_out = jnp.dot(mixed.reshape(-1, HRW), hr_proj, preferred_element_type=jnp.float32).astype(jnp.bfloat16)
        tiles = s_one.reshape(3, NROWS // ROW_DEV, ROW_DEV * COLS, SW // S_HEAD, S_HEAD)
        tile_out = attend(tiles[0], tiles[1], tiles[2], S_HEAD)
        s_out = jnp.dot(tile_out.reshape(-1, SW), s_proj, preferred_element_type=jnp.float32).astype(jnp.bfloat16)
        return jnp.concatenate([hr_out.reshape(NROWS, COLS, HRW), s_out.reshape(NROWS, COLS, SW)], axis=-1)
    merged = lax.map(one_date, (jnp.moveaxis(hr_qkv, 1, 0), jnp.moveaxis(s_qkv, 1, 0), shifts))

    def one_row(items):
        merged_row, valid_row = items
        return temporal(merged_row, valid_row, date_embed, norm_gain)
    result = lax.map(one_row, (jnp.moveaxis(merged, 1, 0), jnp.moveaxis(cloud_valid, 1, 0)))
    return jnp.moveaxis(result, 0, 1)
```

```python
import functools

import jax
import jax.numpy as jnp
from jax import lax
from jax.experimental import pallas as pl
from jax.experimental.pallas import tpu as pltpu
from jax.sharding import Mesh
from jax.sharding import PartitionSpec as P

HRW = 2816
SW = 1024
HR_HEAD = 32
S_HEAD = 64
T_HEAD = 64
WIN = 8
COLS = 16
ROWS = 8
DATES = 16
F = HRW + SW
TOK = ROWS * COLS
LANES = 128
MARGIN = WIN // 2
LOG2E = 1.4426950408889634
OFF = -1e30

SPACE = ("y", "zl", "core")
DATE = ("x", "zh")


def iota2(shape, dim):
    return lax.broadcasted_iota(jnp.int32, shape, dim)


def attend_group(q, k, v, head_dim, bias, scale):
    heads = LANES // head_dim
    head_of = iota2((TOK, LANES), 1) // head_dim
    mine = [head_of == h for h in range(heads)]
    zero = jnp.zeros_like(k)
    k_heads = jnp.concatenate([jnp.where(m, k, zero) for m in mine], axis=0)
    scores = lax.dot_general(
        q, k_heads, (((1,), (1,)), ((), ())), preferred_element_type=jnp.float32
    )
    weights = []
    for h in range(heads):
        one = scores[:, h * TOK : (h + 1) * TOK] * (scale * LOG2E)
        if bias is not None:
            one = one + bias
        top = jnp.max(one, axis=1, keepdims=True)
        weights.append(jnp.exp2(one - top).astype(jnp.bfloat16))
    weights = jnp.concatenate(weights, axis=1)
    v_heads = jnp.concatenate([jnp.where(m, v, zero) for m in mine], axis=0)
    ones = jnp.concatenate([m.astype(jnp.float32) for m in mine], axis=0).astype(jnp.bfloat16)
    both = jnp.dot(
        weights,
        jnp.concatenate([v_heads, ones], axis=1),
        preferred_element_type=jnp.float32,
    )
    return both[:, :LANES] / both[:, LANES:]


def window_kernel(offset_ref, own_ref, below_ref, out_ref, next_ref, stack):
    offset = offset_ref[0]
    stack[:, :TOK] = own_ref[...]
    stack[:, TOK:] = below_ref[...]
    start = pl.multiple_of(offset * COLS, COLS)
    q, k, v = [stack[i, pl.ds(start, TOK), :] for i in range(3)]
    span = COLS
    col_q = iota2((TOK, TOK), 0) % span
    col_k = iota2((TOK, TOK), 1) % span
    win_q = ((col_q - offset + span) % span) // WIN
    win_k = ((col_k - offset + span) % span) // WIN
    bias = jnp.where(win_q == win_k, 0.0, OFF)
    mixed = attend_group(q, k, v, HR_HEAD, bias, 1.0 / HR_HEAD**0.5).astype(jnp.bfloat16)
    src_row = iota2((TOK, TOK), 1) // COLS + offset
    src_col = iota2((TOK, TOK), 1) % COLS
    dst = iota2((TOK, TOK), 0)
    place = jnp.where((dst // ROWS == src_col) & (dst % ROWS == src_row), 1.0, 0.0)
    out_ref[...] = jnp.dot(
        place.astype(jnp.bfloat16), mixed, preferred_element_type=jnp.float32
    ).astype(jnp.bfloat16)
    half = TOK // 2
    src_row = iota2((half, TOK), 1) // COLS + offset
    src_col = iota2((half, TOK), 1) % COLS
    dst = iota2((half, TOK), 0)
    place = jnp.where(
        (dst // MARGIN == src_col) & (dst % MARGIN + ROWS == src_row), 1.0, 0.0
    )
    next_ref[...] = jnp.dot(
        place.astype(jnp.bfloat16), mixed, preferred_element_type=jnp.float32
    ).astype(jnp.bfloat16)


def window_attention(offset, own, below):
    half = TOK // 2
    groups = HRW // LANES
    return pl.pallas_call(
        window_kernel,
        grid=(groups,),
        in_specs=[
            pl.BlockSpec(memory_space=pltpu.SMEM),
            pl.BlockSpec((3, TOK, LANES), lambda i: (0, 0, i)),
            pl.BlockSpec((3, half, LANES), lambda i: (0, 0, i)),
        ],
        out_specs=[
            pl.BlockSpec((TOK, LANES), lambda i: (0, i)),
            pl.BlockSpec((half, LANES), lambda i: (0, i)),
        ],
        out_shape=[
            jax.ShapeDtypeStruct((TOK, HRW), jnp.bfloat16),
            jax.ShapeDtypeStruct((half, HRW), jnp.bfloat16),
        ],
        scratch_shapes=[pltpu.VMEM((3, TOK + half, LANES), jnp.bfloat16)],
        name="window_attention",
    )(offset, own, below)


def tile_kernel(own_ref, out_ref):
    mixed = attend_group(
        own_ref[0], own_ref[1], own_ref[2], S_HEAD, None, 1.0 / S_HEAD**0.5
    ).astype(jnp.bfloat16)
    src = iota2((TOK, TOK), 1)
    dst = iota2((TOK, TOK), 0)
    place = jnp.where((dst // ROWS == src % COLS) & (dst % ROWS == src // COLS), 1.0, 0.0)
    out_ref[...] = jnp.dot(
        place.astype(jnp.bfloat16), mixed, preferred_element_type=jnp.float32
    ).astype(jnp.bfloat16)


def tile_attention(own):
    return pl.pallas_call(
        tile_kernel,
        grid=(SW // LANES,),
        in_specs=[pl.BlockSpec((3, TOK, LANES), lambda i: (0, 0, i))],
        out_specs=pl.BlockSpec((TOK, LANES), lambda i: (0, i)),
        out_shape=jax.ShapeDtypeStruct((TOK, SW), jnp.bfloat16),
        name="tile_attention",
    )(own)


BLOCK = 256
HR_BLOCKS = HRW // BLOCK
S_BLOCKS = SW // BLOCK


def merge_kernel(
    hr_ref, s_ref, hr_w_ref, s_w_ref, valid_ref, embed_ref, gain_ref, out_ref, mixed_ref, out_tmp
):
    step = pl.program_id(0)

    def one_block(projected):
        col = pl.ds(pl.multiple_of(step * BLOCK, BLOCK), BLOCK)
        embed = embed_ref[...].astype(jnp.float32)
        embed = jnp.broadcast_to(embed[:, None, :], (DATES, ROWS, BLOCK)).reshape(TOK, BLOCK)
        joined = (projected.astype(jnp.bfloat16).astype(jnp.float32) + embed).astype(jnp.bfloat16)
        query = iota2((TOK, TOK), 0)
        key = iota2((TOK, TOK), 1)
        keep = (query % ROWS == key % ROWS) & ((valid_ref[...] > 0) | (query == key))
        bias = jnp.where(keep, 0.0, OFF)
        for g in range(BLOCK // LANES):
            part = joined[:, g * LANES : (g + 1) * LANES]
            mixed = part.astype(jnp.float32) + attend_group(
                part, part, part, T_HEAD, bias, 1.0 / T_HEAD
            )
            mixed_ref[step * (BLOCK // LANES) + g] = mixed

    @pl.when(step < HR_BLOCKS)
    def _():
        one_block(
            lax.dot_general(
                hr_ref[...],
                hr_w_ref[...],
                (((1,), (1,)), ((), ())),
                preferred_element_type=jnp.float32,
            )
        )

    @pl.when(step >= HR_BLOCKS)
    def _():
        one_block(jnp.dot(s_ref[...], s_w_ref[...], preferred_element_type=jnp.float32))

    @pl.when(step == HR_BLOCKS + S_BLOCKS - 1)
    def _():
        total = jnp.zeros((TOK, LANES), jnp.float32)
        for g in range(F // LANES):
            total += mixed_ref[g] * mixed_ref[g]
        scale = lax.rsqrt(jnp.sum(total, axis=1, keepdims=True) * (1.0 / F) + 1e-06)
        for g in range(F // LANES):
            lanes = slice(g * LANES, (g + 1) * LANES)
            out_ref[:, lanes] = (mixed_ref[g] * scale * gain_ref[:, lanes]).astype(jnp.bfloat16)


def merge(hr_tokens, s_tokens, hr_weights, s_weights, valid, embed, gain):
    return pl.pallas_call(
        merge_kernel,
        grid=(HR_BLOCKS + S_BLOCKS,),
        in_specs=[
            pl.BlockSpec((TOK, HRW), lambda i: (0, 0)),
            pl.BlockSpec((TOK, SW), lambda i: (0, 0)),
            pl.BlockSpec((BLOCK, HRW), lambda i: (jnp.minimum(i, HR_BLOCKS - 1), 0)),
            pl.BlockSpec((SW, BLOCK), lambda i: (0, jnp.maximum(i - HR_BLOCKS, 0))),
            pl.BlockSpec((1, TOK), lambda i: (0, 0)),
            pl.BlockSpec((DATES, BLOCK), lambda i: (0, i)),
            pl.BlockSpec((1, F), lambda i: (0, 0)),
        ],
        out_specs=pl.BlockSpec((TOK, F), lambda i: (0, 0)),
        out_shape=jax.ShapeDtypeStruct((TOK, F), jnp.bfloat16),
        scratch_shapes=[
            pltpu.VMEM((F // LANES, TOK, LANES), jnp.float32),
            pltpu.VMEM((8, LANES), jnp.float32),
        ],
        compiler_params=pltpu.CompilerParams(vmem_limit_bytes=40 * 2**20),
        name="merge",
    )(hr_tokens, s_tokens, hr_weights, s_weights, valid, embed, gain)


def per_device(hr_qkv, s_qkv, hr_proj, s_proj, shifts, cloud_valid, date_embed, norm_gain):
    space = lax.axis_size(SPACE)
    half = TOK // 2
    own = hr_qkv.reshape(3, TOK, HRW)
    below = lax.ppermute(
        own[:, :half], SPACE, [(i, (i - 1) % space) for i in range(space)]
    )
    hr_weights = lax.all_gather(hr_proj.T, DATE, axis=0, tiled=True)
    s_weights = lax.all_gather(s_proj, DATE, axis=0, tiled=True)

    tile_out = tile_attention(s_qkv.reshape(3, TOK, SW))
    s_tokens = lax.all_to_all(
        tile_out.reshape(COLS, ROWS, SW), DATE, split_axis=0, concat_axis=0, tiled=True
    )

    window_out, passed = window_attention(shifts, own, below)
    above = lax.ppermute(passed, SPACE, [(i, (i + 1) % space) for i in range(space)])
    window_out = window_out.reshape(COLS, ROWS, HRW)
    top = window_out[:, :MARGIN] + above.reshape(COLS, MARGIN, HRW)
    window_out = jnp.concatenate([top, window_out[:, MARGIN:]], axis=1)
    hr_tokens = lax.all_to_all(window_out, DATE, split_axis=0, concat_axis=0, tiled=True)

    out = merge(
        hr_tokens.reshape(TOK, HRW),
        s_tokens.reshape(TOK, SW),
        hr_weights,
        s_weights,
        cloud_valid.reshape(1, TOK),
        date_embed,
        norm_gain.reshape(1, F),
    )
    return out.reshape(DATES, ROWS, 1, F)


def solution(mesh):
    fine = Mesh(mesh.devices.reshape(4, 4, 2, 4, 4), SPACE + DATE)
    in_specs = (
        P(None, DATE, SPACE, None, None),
        P(None, DATE, SPACE, None, None),
        P(None, DATE),
        P(DATE, None),
        P(DATE),
        P(None, SPACE, DATE),
        P(),
        P(),
    )
    out_specs = P(None, SPACE, DATE, None)
    return jax.shard_map(
        per_device, mesh=fine, in_specs=in_specs, out_specs=out_specs, check_vma=False
    )
```

```python
import functools

import jax
import jax.numpy as jnp
from jax import lax
from jax.experimental import pallas as pl
from jax.experimental.pallas import tpu as pltpu
from jax.sharding import Mesh
from jax.sharding import PartitionSpec as P

HRW = 2816
SW = 1024
HR_HEAD = 32
S_HEAD = 64
T_HEAD = 64
WIN = 8
COLS = 16
ROWS = 8
DATES = 16
F = HRW + SW
TOK = ROWS * COLS
LANES = 128
MARGIN = WIN // 2
LOG2E = 1.4426950408889634
OFF = -1e30

SPACE = ("y", "zl", "core")
DATE = ("x", "zh")


def iota2(shape, dim):
    return lax.broadcasted_iota(jnp.int32, shape, dim)


def head_masks(head_dim):
    head_of = iota2((TOK, LANES), 1) // head_dim
    return [head_of == h for h in range(LANES // head_dim)]


def attend_group(q, k, v, masks, ones, bias, scale):
    zero = jnp.zeros_like(k)
    k_heads = jnp.concatenate([jnp.where(m, k, zero) for m in masks], axis=0)
    scores = lax.dot_general(
        q, k_heads, (((1,), (1,)), ((), ())), preferred_element_type=jnp.float32
    )
    weights = []
    for h in range(len(masks)):
        one = scores[:, h * TOK : (h + 1) * TOK] * (scale * LOG2E)
        if bias is not None:
            one = one + bias
        top = jnp.max(one, axis=1, keepdims=True)
        weights.append(jnp.exp2(one - top).astype(jnp.bfloat16))
    weights = jnp.concatenate(weights, axis=1)
    v_heads = jnp.concatenate([jnp.where(m, v, zero) for m in masks], axis=0)
    both = jnp.dot(
        weights,
        jnp.concatenate([v_heads, ones], axis=1),
        preferred_element_type=jnp.float32,
    )
    return both[:, :LANES] / both[:, LANES:]


def ones_of(masks):
    return jnp.concatenate([m.astype(jnp.float32) for m in masks], axis=0).astype(jnp.bfloat16)


def place_rows(place, mixed):
    return jnp.dot(
        jnp.where(place, 1.0, 0.0).astype(jnp.bfloat16),
        mixed,
        preferred_element_type=jnp.float32,
    ).astype(jnp.bfloat16)


WIN_BLOCKS = 2
WIN_LANES = HRW // WIN_BLOCKS


def window_kernel(offset_ref, own_ref, below_ref, out_ref, next_ref, stack, mixed):
    offset = offset_ref[0]
    stack[:, :TOK] = own_ref[...]
    stack[:, TOK:] = below_ref[...]
    start = pl.multiple_of(offset * COLS, COLS)
    col_q = iota2((TOK, TOK), 0) % COLS
    col_k = iota2((TOK, TOK), 1) % COLS
    win_q = ((col_q - offset + COLS) % COLS) // WIN
    win_k = ((col_k - offset + COLS) % COLS) // WIN
    bias = jnp.where(win_q == win_k, 0.0, OFF)
    masks = head_masks(HR_HEAD)
    ones = ones_of(masks)
    for g in range(WIN_LANES // LANES):
        lanes = slice(g * LANES, (g + 1) * LANES)
        q, k, v = [stack[i, pl.ds(start, TOK), lanes] for i in range(3)]
        mixed[:, lanes] = attend_group(
            q, k, v, masks, ones, bias, 1.0 / HR_HEAD**0.5
        ).astype(jnp.bfloat16)
    src_row = iota2((TOK, TOK), 1) // COLS + offset
    src_col = iota2((TOK, TOK), 1) % COLS
    dst = iota2((TOK, TOK), 0)
    out_ref[...] = place_rows(
        (dst // ROWS == src_col) & (dst % ROWS == src_row), mixed[...]
    )
    half = TOK // 2
    src_row = iota2((half, TOK), 1) // COLS + offset
    src_col = iota2((half, TOK), 1) % COLS
    dst = iota2((half, TOK), 0)
    next_ref[...] = place_rows(
        (dst // MARGIN == src_col) & (dst % MARGIN + ROWS == src_row), mixed[...]
    )


def window_attention(offset, own, below):
    half = TOK // 2
    return pl.pallas_call(
        window_kernel,
        grid=(WIN_BLOCKS,),
        in_specs=[
            pl.BlockSpec(memory_space=pltpu.SMEM),
            pl.BlockSpec((3, TOK, WIN_LANES), lambda i: (0, 0, i)),
            pl.BlockSpec((3, half, WIN_LANES), lambda i: (0, 0, i)),
        ],
        out_specs=[
            pl.BlockSpec((TOK, WIN_LANES), lambda i: (0, i)),
            pl.BlockSpec((half, WIN_LANES), lambda i: (0, i)),
        ],
        out_shape=[
            jax.ShapeDtypeStruct((TOK, HRW), jnp.bfloat16),
            jax.ShapeDtypeStruct((half, HRW), jnp.bfloat16),
        ],
        scratch_shapes=[
            pltpu.VMEM((3, TOK + half, WIN_LANES), jnp.bfloat16),
            pltpu.VMEM((TOK, WIN_LANES), jnp.bfloat16),
        ],
        compiler_params=pltpu.CompilerParams(vmem_limit_bytes=24 * 2**20),
        name="window_attention",
    )(offset, own, below)


def tile_kernel(own_ref, out_ref, mixed):
    masks = head_masks(S_HEAD)
    ones = ones_of(masks)
    for g in range(SW // LANES):
        lanes = slice(g * LANES, (g + 1) * LANES)
        q, k, v = [own_ref[i, :, lanes] for i in range(3)]
        mixed[:, lanes] = attend_group(
            q, k, v, masks, ones, None, 1.0 / S_HEAD**0.5
        ).astype(jnp.bfloat16)
    src = iota2((TOK, TOK), 1)
    dst = iota2((TOK, TOK), 0)
    out_ref[...] = place_rows(
        (dst // ROWS == src % COLS) & (dst % ROWS == src // COLS), mixed[...]
    )


def tile_attention(own):
    return pl.pallas_call(
        tile_kernel,
        out_shape=jax.ShapeDtypeStruct((TOK, SW), jnp.bfloat16),
        scratch_shapes=[pltpu.VMEM((TOK, SW), jnp.bfloat16)],
        compiler_params=pltpu.CompilerParams(vmem_limit_bytes=16 * 2**20),
        name="tile_attention",
    )(own)


XS = 4
ZS = 4
SHARD = HRW // DATES
CHUNK = ZS * SHARD
CHUNK_PAD = 768
PIECE = 384
S_SHARD = SW // DATES
S_ROWS = S_SHARD // 2
PIECE_ROWS = SHARD + S_ROWS
NEAR_Y = (0, -1, 1, 2)
NEAR_Z = (-1, 1, 2)
PIECES = 8
LAST = HRW - PIECE
N_BLOCK = 256


def project_kernel(
    place_ref, own_ref, left_ref, right_ref, far_a_ref, far_b_ref, shard_ref, mine_ref, other_ref,
    out_ref, weights, sems,
):
    core, y, zh = place_ref[0], place_ref[1], place_ref[2]
    copies = []

    def fetch(src, piece, part):
        rows = pl.ds(pl.multiple_of(part * SHARD, SHARD), SHARD)
        copies.append(
            pltpu.make_async_copy(src, weights.at[piece, rows, :], sems.at[len(copies)])
        )
        copies[-1].start()

    for j in range(PIECES):
        fetch(shard_ref.at[:, pl.ds(min(j * PIECE, LAST), PIECE)], j, zh)
    for src, c in ((mine_ref, core), (other_ref, 1 - core)):
        for b, dy in enumerate(NEAR_Y):
            for s, dz in enumerate(NEAR_Z):
                fetch(
                    src.at[pl.ds((b * 3 + s) * PIECE_ROWS, SHARD), :],
                    c * 4 + lax.rem(y + dy + 4, 4),
                    lax.rem(zh + dz + 4, 4),
                )
    weights[:, CHUNK:, :] = jnp.zeros((PIECES, CHUNK_PAD - CHUNK, PIECE), jnp.bfloat16)
    tokens = jnp.concatenate(
        [own_ref[...], left_ref[...], right_ref[...], far_a_ref[...], far_b_ref[...]], axis=0
    )
    for copy in copies:
        copy.wait()
    for n in range(CHUNK_PAD // N_BLOCK):
        rows = slice(n * N_BLOCK, (n + 1) * N_BLOCK)
        part = [weights[j, rows, :] for j in range(PIECES - 1)]
        part.append(weights[PIECES - 1, rows, 2 * LANES :])
        result = lax.dot_general(
            tokens,
            jnp.concatenate(part, axis=1),
            (((1,), (1,)), ((), ())),
            preferred_element_type=jnp.float32,
        )
        result = result.reshape(XS, COLS, ROWS, N_BLOCK)
        result = jnp.concatenate([result[b] for b in range(XS)], axis=1)
        out_ref[:, :, rows] = result.astype(jnp.bfloat16)


def project(place, tokens, shard, mine, other):
    vmem = pl.BlockSpec(memory_space=pltpu.VMEM)
    hbm = pl.BlockSpec(memory_space=pl.ANY)
    return pl.pallas_call(
        project_kernel,
        in_specs=[pl.BlockSpec(memory_space=pltpu.SMEM)] + [vmem] * 5 + [hbm] * 3,
        out_specs=vmem,
        out_shape=jax.ShapeDtypeStruct((COLS, XS * ROWS, CHUNK_PAD), jnp.bfloat16),
        scratch_shapes=[
            pltpu.VMEM((PIECES, CHUNK_PAD, PIECE), jnp.bfloat16),
            pltpu.SemaphoreType.DMA((PIECES + 24,)),
        ],
        compiler_params=pltpu.CompilerParams(vmem_limit_bytes=40 * 2**20),
        name="project",
    )(place, *tokens, shard, mine, other)


def s_project_kernel(
    place_ref, tokens_ref, own_ref, left_ref, right_ref, far_a_ref, far_b_ref, out_ref, weights
):
    core, y, zh, x = [place_ref[i] for i in range(4)]
    blocks = [(j, zh) for j in range(PIECES)]
    for c in (core, 1 - core):
        for dy in NEAR_Y:
            for dz in NEAR_Z:
                blocks.append((c * 4 + lax.rem(y + dy + 4, 4), lax.rem(zh + dz + 4, 4)))
    for b, dx in enumerate(NEAR_Y):
        xs = lax.rem(x + dx + 4, 4)
        for i, (j, zs) in enumerate(blocks):
            if b < 3:
                block = (own_ref, left_ref, right_ref)[b][i]
            elif i < 16:
                block = far_a_ref[i]
            else:
                block = far_b_ref[i - 16]
            row = (xs * ZS + zs) * S_SHARD
            for half in range(2):
                rows = pl.ds(pl.multiple_of(row + half * S_ROWS, S_ROWS), S_ROWS)
                weights[j, rows, :] = block[:, half * LANES : (half + 1) * LANES]
    for n in range(SW // N_BLOCK):
        part = jnp.concatenate([weights[2 * n], weights[2 * n + 1]], axis=1)
        out_ref[:, n * N_BLOCK : (n + 1) * N_BLOCK] = jnp.dot(
            tokens_ref[...], part, preferred_element_type=jnp.float32
        ).astype(jnp.bfloat16)


def s_project(place, tokens, raw):
    return pl.pallas_call(
        s_project_kernel,
        in_specs=[pl.BlockSpec(memory_space=pltpu.SMEM)]
        + [pl.BlockSpec(memory_space=pltpu.VMEM)] * 6,
        out_shape=jax.ShapeDtypeStruct((TOK, SW), jnp.bfloat16),
        scratch_shapes=[pltpu.VMEM((PIECES, SW, LANES), jnp.bfloat16)],
        compiler_params=pltpu.CompilerParams(vmem_limit_bytes=16 * 2**20),
        name="s_project",
    )(place, tokens, *raw)


HR_GROUPS = CHUNK_PAD // LANES
GROUPS = XS * HR_GROUPS + SW // LANES
BLOCK_OF = {0: 0, 3: 1, 1: 2, 2: 3}


def merge_kernel(
    hr_ref, s_ref, valid_ref, hr_embed_ref, s_embed_ref, hr_gain_ref, s_gain_ref,
    out_ref, mixed_ref,
):
    query = iota2((TOK, TOK), 0)
    key = iota2((TOK, TOK), 1)
    keep = (query % ROWS == key % ROWS) & ((valid_ref[...] > 0) | (query == key))
    bias = jnp.where(keep, 0.0, OFF)
    masks = head_masks(T_HEAD)
    ones = ones_of(masks)

    def merge_group(projected, embed, group):
        joined = (projected + embed.astype(jnp.float32)[:, None, :]).reshape(TOK, LANES)
        joined = joined.astype(jnp.bfloat16)
        mixed = joined.astype(jnp.float32) + attend_group(
            joined, joined, joined, masks, ones, bias, 1.0 / T_HEAD
        )
        mixed_ref[group] = mixed
        return mixed * mixed

    total = jnp.zeros((TOK, LANES), jnp.float32)
    for xs in range(XS):
        for g in range(HR_GROUPS):
            lanes = slice(g * LANES, (g + 1) * LANES)
            part = hr_ref[xs * ZS : (xs + 1) * ZS, :, lanes].astype(jnp.float32)
            part = part.reshape(ZS, XS, ROWS, LANES)
            part = jnp.concatenate(
                [part[:, BLOCK_OF[(x - xs) % XS]] for x in range(XS)], axis=0
            )
            at = slice(xs * CHUNK_PAD + g * LANES, xs * CHUNK_PAD + (g + 1) * LANES)
            total += merge_group(part, hr_embed_ref[:, at], xs * HR_GROUPS + g)
    for n in range(SW // N_BLOCK):
        cols = slice(n * N_BLOCK, (n + 1) * N_BLOCK)
        part = s_ref[:, cols].astype(jnp.float32).reshape(DATES, ROWS, N_BLOCK)
        for g in range(N_BLOCK // LANES):
            lanes = slice(g * LANES, (g + 1) * LANES)
            at = slice(n * N_BLOCK + g * LANES, n * N_BLOCK + (g + 1) * LANES)
            group = XS * HR_GROUPS + n * (N_BLOCK // LANES) + g
            total += merge_group(part[:, :, lanes], s_embed_ref[:, at], group)
    scale = lax.rsqrt(jnp.sum(total, axis=1, keepdims=True) * (1.0 / F) + 1e-06)
    for xs in range(XS):
        for g in range(HR_GROUPS):
            width = min(LANES, CHUNK - g * LANES)
            at = xs * CHUNK_PAD + g * LANES
            value = mixed_ref[xs * HR_GROUPS + g] * scale * hr_gain_ref[:, at : at + LANES]
            to = xs * CHUNK + g * LANES
            out_ref[:, to : to + width] = value[:, :width].astype(jnp.bfloat16)
    for g in range(SW // LANES):
        lanes = slice(g * LANES, (g + 1) * LANES)
        value = mixed_ref[XS * HR_GROUPS + g] * scale * s_gain_ref[:, lanes]
        out_ref[:, HRW + g * LANES : HRW + (g + 1) * LANES] = value.astype(jnp.bfloat16)


def merge(hr, s_out, valid, embed, gain):
    def padded(array):
        array = array[:, :HRW].reshape(-1, XS, CHUNK)
        return jnp.pad(array, ((0, 0), (0, 0), (0, CHUNK_PAD - CHUNK))).reshape(-1, XS * CHUNK_PAD)

    return pl.pallas_call(
        merge_kernel,
        out_shape=jax.ShapeDtypeStruct((TOK, F), jnp.bfloat16),
        scratch_shapes=[pltpu.VMEM((GROUPS, TOK, LANES), jnp.float32)],
        compiler_params=pltpu.CompilerParams(vmem_limit_bytes=40 * 2**20),
        name="merge",
    )(
        hr, s_out, valid, padded(embed), embed[:, HRW:], padded(gain), gain[:, HRW:]
    )


def ring(x, axis, by):
    size = lax.axis_size(axis)
    return lax.ppermute(x, axis, [(i, (i + by) % size) for i in range(size)])


def after(x, *others):
    return lax.optimization_barrier((x,) + others)[0]


def neighbours(x, axis):
    return ring(x, axis, 1), ring(x, axis, -1)


def opposite(pair, axis):
    half = pair[0].shape[0] // 2
    return ring(pair[0][:half], axis, 1), ring(pair[1][half:], axis, -1)


def per_device(hr_qkv, s_qkv, hr_proj, s_proj, shifts, cloud_valid, date_embed, norm_gain):
    half = TOK // 2
    core, y, zh, x = [lax.axis_index(axis) for axis in ("core", "y", "zh", "x")]
    place = jnp.stack([core, y, zh, x]).astype(jnp.int32)
    own = hr_qkv.reshape(3, TOK, HRW)
    below = ring(own[:, :half], SPACE, -1)

    index = core * 4 + y
    shard = hr_proj.T
    s_shard = s_proj.reshape(2, S_ROWS, PIECES, LANES).transpose(2, 1, 0, 3)
    s_shard = s_shard.reshape(PIECES, S_ROWS, 2 * LANES)
    piece = jnp.concatenate(
        [
            lax.dynamic_slice_in_dim(shard, jnp.minimum(index * PIECE, LAST), PIECE, axis=1),
            jnp.pad(s_shard[index], ((0, 0), (0, LANES))),
        ],
        axis=0,
    )
    near = neighbours(piece, "zh")

    tile_out = tile_attention(s_qkv.reshape(3, TOK, SW))
    below = after(below, tile_out, near)
    window_out, passed = window_attention(shifts, own, below)
    above = ring(passed, SPACE, 1)
    near = after(near, window_out)
    foreign = jnp.concatenate(near + opposite(near, "zh"), axis=0)

    window_out = window_out.reshape(COLS, ROWS, HRW)
    top = window_out[:, :MARGIN] + above.reshape(COLS, MARGIN, HRW)
    window_out = jnp.concatenate([top, window_out[:, MARGIN:]], axis=1).reshape(TOK, HRW)
    beside = neighbours(window_out, "x")
    near = after(neighbours(foreign, "y"), beside)
    far = opposite(beside, "x")
    mine = jnp.concatenate((foreign,) + near + opposite(near, "y"), axis=0)
    mine = after(mine, far)
    other = ring(mine, "core", 1)

    s_tokens = lax.all_to_all(
        tile_out.reshape(COLS, ROWS, SW), DATE, split_axis=0, concat_axis=0, tiled=True
    )
    hr_out = project(place, (window_out,) + beside + far, shard, mine, other)
    hr_out = lax.all_to_all(hr_out, DATE, split_axis=0, concat_axis=0, tiled=True)

    raw = [
        part.reshape(-1, PIECE_ROWS, PIECE)[:, SHARD:, : 2 * LANES] for part in (mine, other)
    ]
    raw = jnp.concatenate([s_shard] + raw, axis=0)
    near = neighbours(raw, "x")
    s_out = s_project(place, s_tokens.reshape(TOK, SW), (raw,) + near + opposite(near, "x"))

    out = merge(
        hr_out,
        s_out,
        cloud_valid.reshape(1, TOK),
        date_embed,
        norm_gain.reshape(1, F),
    )
    return out.reshape(DATES, ROWS, 1, F)


def solution(mesh):
    fine = Mesh(mesh.devices.reshape(4, 4, 2, 4, 4), SPACE + DATE)
    in_specs = (
        P(None, DATE, SPACE, None, None),
        P(None, DATE, SPACE, None, None),
        P(None, DATE),
        P(DATE, None),
        P(DATE),
        P(None, SPACE, DATE),
        P(),
        P(),
    )
    out_specs = P(None, SPACE, DATE, None)
    return jax.shard_map(
        per_device, mesh=fine, in_specs=in_specs, out_specs=out_specs, check_vma=False
    )
```

```python
import functools

import jax
import jax.numpy as jnp
from jax import lax
from jax.experimental import pallas as pl
from jax.experimental.pallas import tpu as pltpu
from jax.sharding import Mesh
from jax.sharding import PartitionSpec as P

HRW = 2816
SW = 1024
HR_HEAD = 32
S_HEAD = 64
T_HEAD = 64
WIN = 8
COLS = 16
ROWS = 8
DATES = 16
F = HRW + SW
TOK = ROWS * COLS
LANES = 128
MARGIN = WIN // 2
LOG2E = 1.4426950408889634
OFF = -1e30

SPACE = ("y", "zl", "core")
DATE = ("x", "zh")


def iota2(shape, dim):
    return lax.broadcasted_iota(jnp.int32, shape, dim)


def head_masks(head_dim):
    head_of = iota2((TOK, LANES), 1) // head_dim
    return [head_of == h for h in range(LANES // head_dim)]


def attend_group(q, k, v, masks, ones, bias, scale):
    zero = jnp.zeros_like(k)
    k_heads = jnp.concatenate([jnp.where(m, k, zero) for m in masks], axis=0)
    scores = lax.dot_general(
        q, k_heads, (((1,), (1,)), ((), ())), preferred_element_type=jnp.float32
    )
    weights = []
    for h in range(len(masks)):
        one = scores[:, h * TOK : (h + 1) * TOK] * (scale * LOG2E)
        if bias is not None:
            one = one + bias
        top = jnp.max(one, axis=1, keepdims=True)
        weights.append(jnp.exp2(one - top).astype(jnp.bfloat16))
    weights = jnp.concatenate(weights, axis=1)
    v_heads = jnp.concatenate([jnp.where(m, v, zero) for m in masks], axis=0)
    both = jnp.dot(
        weights,
        jnp.concatenate([v_heads, ones], axis=1),
        preferred_element_type=jnp.float32,
    )
    return both[:, :LANES] / both[:, LANES:]


def ones_of(masks):
    return jnp.concatenate([m.astype(jnp.float32) for m in masks], axis=0).astype(jnp.bfloat16)


def place_rows(place, mixed):
    return jnp.dot(
        jnp.where(place, 1.0, 0.0).astype(jnp.bfloat16),
        mixed,
        preferred_element_type=jnp.float32,
    ).astype(jnp.bfloat16)


WIN_BLOCKS = 2
WIN_LANES = HRW // WIN_BLOCKS


def window_kernel(offset_ref, own_ref, below_ref, out_ref, next_ref, stack, mixed):
    offset = offset_ref[0]
    stack[:, :TOK] = own_ref[...]
    stack[:, TOK:] = below_ref[...]
    start = pl.multiple_of(offset * COLS, COLS)
    col_q = iota2((TOK, TOK), 0) % COLS
    col_k = iota2((TOK, TOK), 1) % COLS
    win_q = ((col_q - offset + COLS) % COLS) // WIN
    win_k = ((col_k - offset + COLS) % COLS) // WIN
    bias = jnp.where(win_q == win_k, 0.0, OFF)
    masks = head_masks(HR_HEAD)
    ones = ones_of(masks)
    for g in range(WIN_LANES // LANES):
        lanes = slice(g * LANES, (g + 1) * LANES)
        q, k, v = [stack[i, pl.ds(start, TOK), lanes] for i in range(3)]
        mixed[:, lanes] = attend_group(
            q, k, v, masks, ones, bias, 1.0 / HR_HEAD**0.5
        ).astype(jnp.bfloat16)
    src_row = iota2((TOK, TOK), 1) // COLS + offset
    src_col = iota2((TOK, TOK), 1) % COLS
    dst = iota2((TOK, TOK), 0)
    out_ref[...] = place_rows(
        (dst // ROWS == src_col) & (dst % ROWS == src_row), mixed[...]
    )
    half = TOK // 2
    src_row = iota2((half, TOK), 1) // COLS + offset
    src_col = iota2((half, TOK), 1) % COLS
    dst = iota2((half, TOK), 0)
    next_ref[...] = place_rows(
        (dst // MARGIN == src_col) & (dst % MARGIN + ROWS == src_row), mixed[...]
    )


def window_attention(offset, own, below):
    half = TOK // 2
    return pl.pallas_call(
        window_kernel,
        grid=(WIN_BLOCKS,),
        in_specs=[
            pl.BlockSpec(memory_space=pltpu.SMEM),
            pl.BlockSpec((3, TOK, WIN_LANES), lambda i: (0, 0, i)),
            pl.BlockSpec((3, half, WIN_LANES), lambda i: (0, 0, i)),
        ],
        out_specs=[
            pl.BlockSpec((TOK, WIN_LANES), lambda i: (0, i)),
            pl.BlockSpec((half, WIN_LANES), lambda i: (0, i)),
        ],
        out_shape=[
            jax.ShapeDtypeStruct((TOK, HRW), jnp.bfloat16),
            jax.ShapeDtypeStruct((half, HRW), jnp.bfloat16),
        ],
        scratch_shapes=[
            pltpu.VMEM((3, TOK + half, WIN_LANES), jnp.bfloat16),
            pltpu.VMEM((TOK, WIN_LANES), jnp.bfloat16),
        ],
        compiler_params=pltpu.CompilerParams(vmem_limit_bytes=14 * 2**20),
        name="window_attention",
    )(offset, own, below)


def tile_kernel(own_ref, out_ref, mixed):
    masks = head_masks(S_HEAD)
    ones = ones_of(masks)
    for g in range(SW // LANES):
        lanes = slice(g * LANES, (g + 1) * LANES)
        q, k, v = [own_ref[i, :, lanes] for i in range(3)]
        mixed[:, lanes] = attend_group(
            q, k, v, masks, ones, None, 1.0 / S_HEAD**0.5
        ).astype(jnp.bfloat16)
    src = iota2((TOK, TOK), 1)
    dst = iota2((TOK, TOK), 0)
    out_ref[...] = place_rows(
        (dst // ROWS == src % COLS) & (dst % ROWS == src // COLS), mixed[...]
    )


def tile_attention(own):
    return pl.pallas_call(
        tile_kernel,
        out_shape=jax.ShapeDtypeStruct((TOK, SW), jnp.bfloat16),
        scratch_shapes=[pltpu.VMEM((TOK, SW), jnp.bfloat16)],
        compiler_params=pltpu.CompilerParams(vmem_limit_bytes=12 * 2**20),
        name="tile_attention",
    )(own)


XS = 4
ZS = 4
SHARD = HRW // DATES
CHUNK = ZS * SHARD
CHUNK_PAD = 768
PIECE = 384
S_SHARD = SW // DATES
S_ROWS = S_SHARD // 2
PIECE_ROWS = SHARD + S_ROWS
NEAR_Y = (0, -1, 1, 2)
NEAR_Z = (-1, 1, 2)
PIECES = 8
LAST = HRW - PIECE
N_BLOCK = 256


def project_kernel(
    place_ref, own_ref, left_ref, right_ref, far_a_ref, far_b_ref, shard_ref, mine_ref, other_ref,
    out_ref, tokens, weights, sems,
):
    core, y, zh = place_ref[0], place_ref[1], place_ref[2]
    copies = []
    row = 0
    for src in (own_ref, left_ref, right_ref, far_a_ref, far_b_ref):
        copies.append(
            pltpu.make_async_copy(
                src, tokens.at[pl.ds(row, src.shape[0]), :], sems.at[len(copies)]
            )
        )
        copies[-1].start()
        row += src.shape[0]

    def fetch(src, piece, part):
        rows = pl.ds(pl.multiple_of(part * SHARD, SHARD), SHARD)
        copies.append(
            pltpu.make_async_copy(src, weights.at[piece, rows, :], sems.at[len(copies)])
        )
        copies[-1].start()

    for j in range(PIECES):
        fetch(shard_ref.at[:, pl.ds(min(j * PIECE, LAST), PIECE)], j, zh)
    for src, c in ((mine_ref, core), (other_ref, 1 - core)):
        for b, dy in enumerate(NEAR_Y):
            for s, dz in enumerate(NEAR_Z):
                fetch(
                    src.at[pl.ds((b * 3 + s) * PIECE_ROWS, SHARD), :],
                    c * 4 + lax.rem(y + dy + 4, 4),
                    lax.rem(zh + dz + 4, 4),
                )
    weights[:, CHUNK:, :] = jnp.zeros((PIECES, CHUNK_PAD - CHUNK, PIECE), jnp.bfloat16)
    for copy in copies:
        copy.wait()
    for n in range(CHUNK_PAD // N_BLOCK):
        rows = slice(n * N_BLOCK, (n + 1) * N_BLOCK)
        part = [weights[j, rows, :] for j in range(PIECES - 1)]
        part.append(weights[PIECES - 1, rows, 2 * LANES :])
        result = lax.dot_general(
            tokens[...],
            jnp.concatenate(part, axis=1),
            (((1,), (1,)), ((), ())),
            preferred_element_type=jnp.float32,
        )
        result = result.reshape(XS, COLS, ROWS, N_BLOCK)
        result = jnp.concatenate([result[b] for b in range(XS)], axis=1)
        out_ref[:, :, rows] = result.astype(jnp.bfloat16)


def project(place, tokens, shard, mine, other):
    vmem = pl.BlockSpec(memory_space=pltpu.VMEM)
    hbm = pl.BlockSpec(memory_space=pltpu.HBM)
    anywhere = pl.BlockSpec(memory_space=pl.ANY)
    return pl.pallas_call(
        project_kernel,
        in_specs=[pl.BlockSpec(memory_space=pltpu.SMEM)] + [hbm] * 5 + [anywhere] * 3,
        out_specs=vmem,
        out_shape=jax.ShapeDtypeStruct((COLS, XS * ROWS, CHUNK_PAD), jnp.bfloat16),
        scratch_shapes=[
            pltpu.VMEM((XS * TOK, HRW), jnp.bfloat16),
            pltpu.VMEM((PIECES, CHUNK_PAD, PIECE), jnp.bfloat16),
            pltpu.SemaphoreType.DMA((PIECES + 24 + 5,)),
        ],
        compiler_params=pltpu.CompilerParams(vmem_limit_bytes=20 * 2**20),
        name="project",
    )(place, *tokens, shard, mine, other)


def s_project_kernel(place_ref, tokens_ref, mine_ref, other_ref, out_ref, weights):
    core, y, zh, x = [place_ref[i] for i in range(4)]
    for raw_ref, c in ((mine_ref, core), (other_ref, 1 - core)):
        blocks = [(c * 4 + i, zh) for i in range(4)]
        for dy in NEAR_Y:
            for dz in NEAR_Z:
                blocks.append((c * 4 + lax.rem(y + dy + 4, 4), lax.rem(zh + dz + 4, 4)))
        for b, dx in enumerate(NEAR_Y):
            xs = lax.rem(x + dx + 4, 4)
            for i, (j, zs) in enumerate(blocks):
                block = raw_ref[b * len(blocks) + i]
                row = (xs * ZS + zs) * S_SHARD
                for half in range(2):
                    rows = pl.ds(pl.multiple_of(row + half * S_ROWS, S_ROWS), S_ROWS)
                    weights[j, rows, :] = block[:, half * LANES : (half + 1) * LANES]
    for n in range(SW // N_BLOCK):
        part = jnp.concatenate([weights[2 * n], weights[2 * n + 1]], axis=1)
        out_ref[:, n * N_BLOCK : (n + 1) * N_BLOCK] = jnp.dot(
            tokens_ref[...], part, preferred_element_type=jnp.float32
        ).astype(jnp.bfloat16)


def s_project(place, tokens, mine, other):
    return pl.pallas_call(
        s_project_kernel,
        in_specs=[pl.BlockSpec(memory_space=pltpu.SMEM)]
        + [pl.BlockSpec(memory_space=pltpu.VMEM)] * 3,
        out_shape=jax.ShapeDtypeStruct((TOK, SW), jnp.bfloat16),
        scratch_shapes=[pltpu.VMEM((PIECES, SW, LANES), jnp.bfloat16)],
        compiler_params=pltpu.CompilerParams(vmem_limit_bytes=12 * 2**20),
        name="s_project",
    )(place, tokens, mine, other)


HR_GROUPS = CHUNK_PAD // LANES
GROUPS = XS * HR_GROUPS + SW // LANES
BLOCK_OF = {0: 0, 3: 1, 1: 2, 2: 3}


def merge_kernel(
    hr_ref, s_ref, valid_ref, hr_embed_ref, s_embed_ref, hr_gain_ref, s_gain_ref,
    out_ref, mixed_ref,
):
    query = iota2((TOK, TOK), 0)
    key = iota2((TOK, TOK), 1)
    keep = (query % ROWS == key % ROWS) & ((valid_ref[...] > 0) | (query == key))
    bias = jnp.where(keep, 0.0, OFF)
    masks = head_masks(T_HEAD)
    ones = ones_of(masks)

    def merge_group(projected, embed, group):
        joined = (projected + embed.astype(jnp.float32)[:, None, :]).reshape(TOK, LANES)
        joined = joined.astype(jnp.bfloat16)
        mixed = joined.astype(jnp.float32) + attend_group(
            joined, joined, joined, masks, ones, bias, 1.0 / T_HEAD
        )
        mixed_ref[group] = mixed
        return mixed * mixed

    total = jnp.zeros((TOK, LANES), jnp.float32)
    for xs in range(XS):
        for g in range(HR_GROUPS):
            lanes = slice(g * LANES, (g + 1) * LANES)
            part = hr_ref[xs * ZS : (xs + 1) * ZS, :, lanes].astype(jnp.float32)
            part = part.reshape(ZS, XS, ROWS, LANES)
            part = jnp.concatenate(
                [part[:, BLOCK_OF[(x - xs) % XS]] for x in range(XS)], axis=0
            )
            at = slice(xs * CHUNK_PAD + g * LANES, xs * CHUNK_PAD + (g + 1) * LANES)
            total += merge_group(part, hr_embed_ref[:, at], xs * HR_GROUPS + g)
    for n in range(SW // N_BLOCK):
        cols = slice(n * N_BLOCK, (n + 1) * N_BLOCK)
        part = s_ref[:, cols].astype(jnp.float32).reshape(DATES, ROWS, N_BLOCK)
        for g in range(N_BLOCK // LANES):
            lanes = slice(g * LANES, (g + 1) * LANES)
            at = slice(n * N_BLOCK + g * LANES, n * N_BLOCK + (g + 1) * LANES)
            group = XS * HR_GROUPS + n * (N_BLOCK // LANES) + g
            total += merge_group(part[:, :, lanes], s_embed_ref[:, at], group)
    scale = lax.rsqrt(jnp.sum(total, axis=1, keepdims=True) * (1.0 / F) + 1e-06)
    for xs in range(XS):
        for g in range(HR_GROUPS):
            width = min(LANES, CHUNK - g * LANES)
            at = xs * CHUNK_PAD + g * LANES
            value = mixed_ref[xs * HR_GROUPS + g] * scale * hr_gain_ref[:, at : at + LANES]
            to = xs * CHUNK + g * LANES
            out_ref[:, to : to + width] = value[:, :width].astype(jnp.bfloat16)
    for g in range(SW // LANES):
        lanes = slice(g * LANES, (g + 1) * LANES)
        value = mixed_ref[XS * HR_GROUPS + g] * scale * s_gain_ref[:, lanes]
        out_ref[:, HRW + g * LANES : HRW + (g + 1) * LANES] = value.astype(jnp.bfloat16)


def merge(hr, s_out, valid, embed, gain):
    def padded(array):
        array = array[:, :HRW].reshape(-1, XS, CHUNK)
        return jnp.pad(array, ((0, 0), (0, 0), (0, CHUNK_PAD - CHUNK))).reshape(-1, XS * CHUNK_PAD)

    return pl.pallas_call(
        merge_kernel,
        out_shape=jax.ShapeDtypeStruct((TOK, F), jnp.bfloat16),
        scratch_shapes=[pltpu.VMEM((GROUPS, TOK, LANES), jnp.float32)],
        compiler_params=pltpu.CompilerParams(vmem_limit_bytes=16 * 2**20),
        name="merge",
    )(
        hr, s_out, valid, padded(embed), embed[:, HRW:], padded(gain), gain[:, HRW:]
    )


def ring(x, axis, by):
    size = lax.axis_size(axis)
    return lax.ppermute(x, axis, [(i, (i + by) % size) for i in range(size)])


def after(x, *others):
    return lax.optimization_barrier((x,) + others)[0]


def neighbours(x, axis):
    return ring(x, axis, 1), ring(x, axis, -1)


def opposite(pair, axis):
    half = pair[0].shape[0] // 2
    return ring(pair[0][:half], axis, 1), ring(pair[1][half:], axis, -1)


def per_device(hr_qkv, s_qkv, hr_proj, s_proj, shifts, cloud_valid, date_embed, norm_gain):
    half = TOK // 2
    core, y, zh, x = [lax.axis_index(axis) for axis in ("core", "y", "zh", "x")]
    place = jnp.stack([core, y, zh, x]).astype(jnp.int32)
    own = hr_qkv.reshape(3, TOK, HRW)
    below = ring(own[:, :half], SPACE, -1)

    index = core * 4 + y
    shard = hr_proj.T
    s_shard = s_proj.reshape(2, S_ROWS, PIECES, LANES).transpose(2, 1, 0, 3)
    s_shard = s_shard.reshape(PIECES, S_ROWS, 2 * LANES)
    piece = jnp.concatenate(
        [
            lax.dynamic_slice_in_dim(shard, jnp.minimum(index * PIECE, LAST), PIECE, axis=1),
            jnp.pad(s_shard[index], ((0, 0), (0, LANES))),
        ],
        axis=0,
    )
    near = neighbours(piece, "zh")

    tile_out = tile_attention(s_qkv.reshape(3, TOK, SW))
    s_tokens = lax.all_to_all(
        tile_out.reshape(COLS, ROWS, SW), DATE, split_axis=0, concat_axis=0, tiled=True
    )
    window_out, passed = window_attention(shifts, own, below)
    above = ring(after(passed, near), SPACE, 1)
    near = after(near, window_out, s_tokens)
    foreign = jnp.concatenate(near + opposite(near, "zh"), axis=0)

    window_out = window_out.reshape(COLS, ROWS, HRW)
    top = window_out[:, :MARGIN] + above.reshape(COLS, MARGIN, HRW)
    window_out = jnp.concatenate([top, window_out[:, MARGIN:]], axis=1).reshape(TOK, HRW)
    beside = neighbours(window_out, "x")
    near = after(neighbours(foreign, "y"), beside)
    far = opposite(beside, "x")
    mine = jnp.concatenate((foreign,) + near + opposite(near, "y"), axis=0)
    mine = after(mine, far)
    other = ring(mine, "core", 1)

    hr_out = project(place, (window_out,) + beside + far, shard, mine, other)
    raw = after(mine, hr_out).reshape(-1, PIECE_ROWS, PIECE)[:, SHARD:, : 2 * LANES]
    hr_out = lax.all_to_all(hr_out, DATE, split_axis=0, concat_axis=0, tiled=True)

    raw = jnp.concatenate([lax.dynamic_slice_in_dim(s_shard, core * 4, 4), raw], axis=0)
    near = neighbours(raw, "x")
    raw = jnp.concatenate((raw,) + near + opposite(near, "x"), axis=0)
    s_out = s_project(place, s_tokens.reshape(TOK, SW), raw, ring(raw, "core", 1))

    out = merge(
        hr_out,
        s_out,
        cloud_valid.reshape(1, TOK),
        date_embed,
        norm_gain.reshape(1, F),
    )
    return out.reshape(DATES, ROWS, 1, F)


def solution(mesh):
    fine = Mesh(mesh.devices.reshape(4, 4, 2, 4, 4), SPACE + DATE)
    in_specs = (
        P(None, DATE, SPACE, None, None),
        P(None, DATE, SPACE, None, None),
        P(None, DATE),
        P(DATE, None),
        P(DATE),
        P(None, SPACE, DATE),
        P(),
        P(),
    )
    out_specs = P(None, SPACE, DATE, None)
    return jax.shard_map(
        per_device, mesh=fine, in_specs=in_specs, out_specs=out_specs, check_vma=False
    )
```

```python
import functools

import jax
import jax.numpy as jnp
from jax import lax
from jax.experimental import pallas as pl
from jax.experimental.pallas import tpu as pltpu
from jax.sharding import Mesh
from jax.sharding import PartitionSpec as P

HRW = 2816
SW = 1024
HR_HEAD = 32
S_HEAD = 64
T_HEAD = 64
WIN = 8
COLS = 16
ROWS = 8
DATES = 16
F = HRW + SW
TOK = ROWS * COLS
LANES = 128
MARGIN = WIN // 2
LOG2E = 1.4426950408889634
OFF = -1e30

SPACE = ("y", "zl", "core")
DATE = ("x", "zh")


def iota2(shape, dim):
    return lax.broadcasted_iota(jnp.int32, shape, dim)


def head_masks(head_dim):
    head_of = iota2((TOK, LANES), 1) // head_dim
    return [head_of == h for h in range(LANES // head_dim)]


def attend_group(q, k, v, masks, ones, bias, scale):
    zero = jnp.zeros_like(k)
    k_heads = jnp.concatenate([jnp.where(m, k, zero) for m in masks], axis=0)
    scores = lax.dot_general(
        q, k_heads, (((1,), (1,)), ((), ())), preferred_element_type=jnp.float32
    )
    weights = []
    for h in range(len(masks)):
        one = scores[:, h * TOK : (h + 1) * TOK] * (scale * LOG2E)
        if bias is not None:
            one = one + bias
        top = jnp.max(one, axis=1, keepdims=True)
        weights.append(jnp.exp2(one - top).astype(jnp.bfloat16))
    weights = jnp.concatenate(weights, axis=1)
    v_heads = jnp.concatenate([jnp.where(m, v, zero) for m in masks], axis=0)
    both = jnp.dot(
        weights,
        jnp.concatenate([v_heads, ones], axis=1),
        preferred_element_type=jnp.float32,
    )
    return both[:, :LANES] / both[:, LANES:]


def ones_of(masks):
    return jnp.concatenate([m.astype(jnp.float32) for m in masks], axis=0).astype(jnp.bfloat16)


def place_rows(place, mixed):
    return jnp.dot(
        jnp.where(place, 1.0, 0.0).astype(jnp.bfloat16),
        mixed,
        preferred_element_type=jnp.float32,
    ).astype(jnp.bfloat16)


WIN_BLOCKS = 2
WIN_LANES = HRW // WIN_BLOCKS


def window_kernel(offset_ref, own_ref, below_ref, out_ref, next_ref, stack, mixed):
    offset = offset_ref[0]
    stack[:, :TOK] = own_ref[...]
    stack[:, TOK:] = below_ref[...]
    start = pl.multiple_of(offset * COLS, COLS)
    col_q = iota2((TOK, TOK), 0) % COLS
    col_k = iota2((TOK, TOK), 1) % COLS
    win_q = ((col_q - offset + COLS) % COLS) // WIN
    win_k = ((col_k - offset + COLS) % COLS) // WIN
    bias = jnp.where(win_q == win_k, 0.0, OFF)
    masks = head_masks(HR_HEAD)
    ones = ones_of(masks)
    for g in range(WIN_LANES // LANES):
        lanes = slice(g * LANES, (g + 1) * LANES)
        q, k, v = [stack[i, pl.ds(start, TOK), lanes] for i in range(3)]
        mixed[:, lanes] = attend_group(
            q, k, v, masks, ones, bias, 1.0 / HR_HEAD**0.5
        ).astype(jnp.bfloat16)
    src_row = iota2((TOK, TOK), 1) // COLS + offset
    src_col = iota2((TOK, TOK), 1) % COLS
    dst = iota2((TOK, TOK), 0)
    out_ref[...] = place_rows(
        (dst // ROWS == src_col) & (dst % ROWS == src_row), mixed[...]
    )
    half = TOK // 2
    src_row = iota2((half, TOK), 1) // COLS + offset
    src_col = iota2((half, TOK), 1) % COLS
    dst = iota2((half, TOK), 0)
    next_ref[...] = place_rows(
        (dst // MARGIN == src_col) & (dst % MARGIN + ROWS == src_row), mixed[...]
    )


def window_attention(offset, own, below):
    half = TOK // 2
    return pl.pallas_call(
        window_kernel,
        grid=(WIN_BLOCKS,),
        in_specs=[
            pl.BlockSpec(memory_space=pltpu.SMEM),
            pl.BlockSpec((3, TOK, WIN_LANES), lambda i: (0, 0, i)),
            pl.BlockSpec((3, half, WIN_LANES), lambda i: (0, 0, i)),
        ],
        out_specs=[
            pl.BlockSpec((TOK, WIN_LANES), lambda i: (0, i)),
            pl.BlockSpec((half, WIN_LANES), lambda i: (0, i)),
        ],
        out_shape=[
            jax.ShapeDtypeStruct((TOK, HRW), jnp.bfloat16),
            jax.ShapeDtypeStruct((half, HRW), jnp.bfloat16),
        ],
        scratch_shapes=[
            pltpu.VMEM((3, TOK + half, WIN_LANES), jnp.bfloat16),
            pltpu.VMEM((TOK, WIN_LANES), jnp.bfloat16),
        ],
        compiler_params=pltpu.CompilerParams(vmem_limit_bytes=14 * 2**20),
        name="window_attention",
    )(offset, own, below)


def tile_kernel(own_ref, out_ref, mixed):
    masks = head_masks(S_HEAD)
    ones = ones_of(masks)
    for g in range(SW // LANES):
        lanes = slice(g * LANES, (g + 1) * LANES)
        q, k, v = [own_ref[i, :, lanes] for i in range(3)]
        mixed[:, lanes] = attend_group(
            q, k, v, masks, ones, None, 1.0 / S_HEAD**0.5
        ).astype(jnp.bfloat16)
    src = iota2((TOK, TOK), 1)
    dst = iota2((TOK, TOK), 0)
    out_ref[...] = place_rows(
        (dst // ROWS == src % COLS) & (dst % ROWS == src // COLS), mixed[...]
    )


def tile_attention(own):
    return pl.pallas_call(
        tile_kernel,
        out_shape=jax.ShapeDtypeStruct((TOK, SW), jnp.bfloat16),
        scratch_shapes=[pltpu.VMEM((TOK, SW), jnp.bfloat16)],
        compiler_params=pltpu.CompilerParams(vmem_limit_bytes=12 * 2**20),
        name="tile_attention",
    )(own)


XS = 4
ZS = 4
SHARD = HRW // DATES
CHUNK = ZS * SHARD
CHUNK_PAD = 768
PIECE = 384
S_SHARD = SW // DATES
S_ROWS = S_SHARD // 2
PIECE_ROWS = SHARD + S_ROWS
NEAR_Y = (0, -1, 1, 2)
NEAR_Z = (-1, 1, 2)
PIECES = 8
LAST = HRW - PIECE
N_BLOCK = 256


def project_kernel(
    place_ref, own_ref, left_ref, right_ref, far_a_ref, far_b_ref, shard_ref, mine_ref, other_ref,
    out_ref, tokens, weights, sems,
):
    core, y, zh = place_ref[0], place_ref[1], place_ref[2]
    copies = []
    row = 0
    for src in (own_ref, left_ref, right_ref, far_a_ref, far_b_ref):
        copies.append(
            pltpu.make_async_copy(
                src, tokens.at[pl.ds(row, src.shape[0]), :], sems.at[len(copies)]
            )
        )
        copies[-1].start()
        row += src.shape[0]

    def fetch(src, piece, part):
        rows = pl.ds(pl.multiple_of(part * SHARD, SHARD), SHARD)
        copies.append(
            pltpu.make_async_copy(src, weights.at[piece, rows, :], sems.at[len(copies)])
        )
        copies[-1].start()

    for j in range(PIECES):
        fetch(shard_ref.at[:, pl.ds(min(j * PIECE, LAST), PIECE)], j, zh)
    for src, c in ((mine_ref, core), (other_ref, 1 - core)):
        for b, dy in enumerate(NEAR_Y):
            for s, dz in enumerate(NEAR_Z):
                fetch(
                    src.at[pl.ds((b * 3 + s) * PIECE_ROWS, SHARD), :],
                    c * 4 + lax.rem(y + dy + 4, 4),
                    lax.rem(zh + dz + 4, 4),
                )
    weights[:, CHUNK:, :] = jnp.zeros((PIECES, CHUNK_PAD - CHUNK, PIECE), jnp.bfloat16)
    for copy in copies:
        copy.wait()
    for n in range(CHUNK_PAD // N_BLOCK):
        rows = slice(n * N_BLOCK, (n + 1) * N_BLOCK)
        part = [weights[j, rows, :] for j in range(PIECES - 1)]
        part.append(weights[PIECES - 1, rows, 2 * LANES :])
        result = lax.dot_general(
            tokens[...],
            jnp.concatenate(part, axis=1),
            (((1,), (1,)), ((), ())),
            preferred_element_type=jnp.float32,
        )
        result = result.reshape(XS, COLS, ROWS, N_BLOCK)
        result = jnp.concatenate([result[b] for b in range(XS)], axis=1)
        out_ref[:, :, rows] = result.astype(jnp.bfloat16)


def project(place, tokens, shard, mine, other):
    vmem = pl.BlockSpec(memory_space=pltpu.VMEM)
    hbm = pl.BlockSpec(memory_space=pltpu.HBM)
    anywhere = pl.BlockSpec(memory_space=pl.ANY)
    return pl.pallas_call(
        project_kernel,
        in_specs=[pl.BlockSpec(memory_space=pltpu.SMEM)] + [hbm] * 5 + [anywhere] * 3,
        out_specs=vmem,
        out_shape=jax.ShapeDtypeStruct((COLS, XS * ROWS, CHUNK_PAD), jnp.bfloat16),
        scratch_shapes=[
            pltpu.VMEM((XS * TOK, HRW), jnp.bfloat16),
            pltpu.VMEM((PIECES, CHUNK_PAD, PIECE), jnp.bfloat16),
            pltpu.SemaphoreType.DMA((PIECES + 24 + 5,)),
        ],
        compiler_params=pltpu.CompilerParams(vmem_limit_bytes=20 * 2**20),
        name="project",
    )(place, *tokens, shard, mine, other)


def s_project_kernel(
    place_ref, tokens_ref, own_ref, left_ref, right_ref, far_a_ref, far_b_ref, out_ref, weights
):
    core, y, zh, x = [place_ref[i] for i in range(4)]
    blocks = [(j, zh) for j in range(PIECES)]
    for c in (core, 1 - core):
        for dy in NEAR_Y:
            for dz in NEAR_Z:
                blocks.append((c * 4 + lax.rem(y + dy + 4, 4), lax.rem(zh + dz + 4, 4)))
    for b, dx in enumerate(NEAR_Y):
        xs = lax.rem(x + dx + 4, 4)
        for i, (j, zs) in enumerate(blocks):
            if b < 3:
                block = (own_ref, left_ref, right_ref)[b][i]
            elif i < 16:
                block = far_a_ref[i]
            else:
                block = far_b_ref[i - 16]
            row = (xs * ZS + zs) * S_SHARD
            for half in range(2):
                rows = pl.ds(pl.multiple_of(row + half * S_ROWS, S_ROWS), S_ROWS)
                weights[j, rows, :] = block[:, half * LANES : (half + 1) * LANES]
    for n in range(SW // N_BLOCK):
        part = jnp.concatenate([weights[2 * n], weights[2 * n + 1]], axis=1)
        out_ref[:, n * N_BLOCK : (n + 1) * N_BLOCK] = jnp.dot(
            tokens_ref[...], part, preferred_element_type=jnp.float32
        ).astype(jnp.bfloat16)


def s_project(place, tokens, raw):
    return pl.pallas_call(
        s_project_kernel,
        in_specs=[pl.BlockSpec(memory_space=pltpu.SMEM)]
        + [pl.BlockSpec(memory_space=pltpu.VMEM)] * 6,
        out_shape=jax.ShapeDtypeStruct((TOK, SW), jnp.bfloat16),
        scratch_shapes=[pltpu.VMEM((PIECES, SW, LANES), jnp.bfloat16)],
        compiler_params=pltpu.CompilerParams(vmem_limit_bytes=12 * 2**20),
        name="s_project",
    )(place, tokens, *raw)


HR_GROUPS = CHUNK_PAD // LANES
GROUPS = XS * HR_GROUPS + SW // LANES
BLOCK_OF = {0: 0, 3: 1, 1: 2, 2: 3}


def merge_kernel(
    hr_ref, s_ref, valid_ref, hr_embed_ref, s_embed_ref, hr_gain_ref, s_gain_ref,
    out_ref, mixed_ref,
):
    query = iota2((TOK, TOK), 0)
    key = iota2((TOK, TOK), 1)
    keep = (query % ROWS == key % ROWS) & ((valid_ref[...] > 0) | (query == key))
    bias = jnp.where(keep, 0.0, OFF)
    masks = head_masks(T_HEAD)
    ones = ones_of(masks)

    def merge_group(projected, embed, group):
        joined = (projected + embed.astype(jnp.float32)[:, None, :]).reshape(TOK, LANES)
        joined = joined.astype(jnp.bfloat16)
        mixed = joined.astype(jnp.float32) + attend_group(
            joined, joined, joined, masks, ones, bias, 1.0 / T_HEAD
        )
        mixed_ref[group] = mixed
        return mixed * mixed

    total = jnp.zeros((TOK, LANES), jnp.float32)
    for xs in range(XS):
        for g in range(HR_GROUPS):
            lanes = slice(g * LANES, (g + 1) * LANES)
            part = hr_ref[xs * ZS : (xs + 1) * ZS, :, lanes].astype(jnp.float32)
            part = part.reshape(ZS, XS, ROWS, LANES)
            part = jnp.concatenate(
                [part[:, BLOCK_OF[(x - xs) % XS]] for x in range(XS)], axis=0
            )
            at = slice(xs * CHUNK_PAD + g * LANES, xs * CHUNK_PAD + (g + 1) * LANES)
            total += merge_group(part, hr_embed_ref[:, at], xs * HR_GROUPS + g)
    for n in range(SW // N_BLOCK):
        cols = slice(n * N_BLOCK, (n + 1) * N_BLOCK)
        part = s_ref[:, cols].astype(jnp.float32).reshape(DATES, ROWS, N_BLOCK)
        for g in range(N_BLOCK // LANES):
            lanes = slice(g * LANES, (g + 1) * LANES)
            at = slice(n * N_BLOCK + g * LANES, n * N_BLOCK + (g + 1) * LANES)
            group = XS * HR_GROUPS + n * (N_BLOCK // LANES) + g
            total += merge_group(part[:, :, lanes], s_embed_ref[:, at], group)
    scale = lax.rsqrt(jnp.sum(total, axis=1, keepdims=True) * (1.0 / F) + 1e-06)
    for xs in range(XS):
        for g in range(HR_GROUPS):
            width = min(LANES, CHUNK - g * LANES)
            at = xs * CHUNK_PAD + g * LANES
            value = mixed_ref[xs * HR_GROUPS + g] * scale * hr_gain_ref[:, at : at + LANES]
            to = xs * CHUNK + g * LANES
            out_ref[:, to : to + width] = value[:, :width].astype(jnp.bfloat16)
    for g in range(SW // LANES):
        lanes = slice(g * LANES, (g + 1) * LANES)
        value = mixed_ref[XS * HR_GROUPS + g] * scale * s_gain_ref[:, lanes]
        out_ref[:, HRW + g * LANES : HRW + (g + 1) * LANES] = value.astype(jnp.bfloat16)


def merge(hr, s_out, valid, embed, gain):
    def padded(array):
        array = array[:, :HRW].reshape(-1, XS, CHUNK)
        return jnp.pad(array, ((0, 0), (0, 0), (0, CHUNK_PAD - CHUNK))).reshape(-1, XS * CHUNK_PAD)

    return pl.pallas_call(
        merge_kernel,
        out_shape=jax.ShapeDtypeStruct((TOK, F), jnp.bfloat16),
        scratch_shapes=[pltpu.VMEM((GROUPS, TOK, LANES), jnp.float32)],
        compiler_params=pltpu.CompilerParams(vmem_limit_bytes=16 * 2**20),
        name="merge",
    )(
        hr, s_out, valid, padded(embed), embed[:, HRW:], padded(gain), gain[:, HRW:]
    )


def ring(x, axis, by):
    size = lax.axis_size(axis)
    return lax.ppermute(x, axis, [(i, (i + by) % size) for i in range(size)])


def after(x, *others):
    return lax.optimization_barrier((x,) + others)[0]


def neighbours(x, axis):
    return ring(x, axis, 1), ring(x, axis, -1)


def opposite(pair, axis):
    half = pair[0].shape[0] // 2
    return ring(pair[0][:half], axis, 1), ring(pair[1][half:], axis, -1)


def per_device(hr_qkv, s_qkv, hr_proj, s_proj, shifts, cloud_valid, date_embed, norm_gain):
    half = TOK // 2
    core, y, zh, x = [lax.axis_index(axis) for axis in ("core", "y", "zh", "x")]
    place = jnp.stack([core, y, zh, x]).astype(jnp.int32)
    own = hr_qkv.reshape(3, TOK, HRW)
    below = ring(own[:, :half], SPACE, -1)

    index = core * 4 + y
    shard = hr_proj.T
    s_shard = s_proj.reshape(2, S_ROWS, PIECES, LANES).transpose(2, 1, 0, 3)
    s_shard = s_shard.reshape(PIECES, S_ROWS, 2 * LANES)
    piece = jnp.concatenate(
        [
            lax.dynamic_slice_in_dim(shard, jnp.minimum(index * PIECE, LAST), PIECE, axis=1),
            jnp.pad(s_shard[index], ((0, 0), (0, LANES))),
        ],
        axis=0,
    )
    near = neighbours(piece, "zh")

    tile_out = tile_attention(s_qkv.reshape(3, TOK, SW))
    below = after(below, tile_out)
    window_out, passed = window_attention(shifts, own, below)
    above = ring(after(passed, near), SPACE, 1)
    near = after(near, window_out)
    foreign = jnp.concatenate(near + opposite(near, "zh"), axis=0)

    window_out = window_out.reshape(COLS, ROWS, HRW)
    top = window_out[:, :MARGIN] + above.reshape(COLS, MARGIN, HRW)
    window_out = jnp.concatenate([top, window_out[:, MARGIN:]], axis=1).reshape(TOK, HRW)
    beside = neighbours(window_out, "x")
    s_tokens = lax.all_to_all(
        after(tile_out, foreign).reshape(COLS, ROWS, SW),
        DATE,
        split_axis=0,
        concat_axis=0,
        tiled=True,
    )
    near = after(neighbours(foreign, "y"), beside)
    far = opposite(beside, "x")
    mine = jnp.concatenate((foreign,) + near + opposite(near, "y"), axis=0)
    mine = after(mine, far, s_tokens)
    other = ring(mine, "core", 1)

    hr_out = project(place, (window_out,) + beside + far, shard, mine, other)
    hr_out = lax.all_to_all(hr_out, DATE, split_axis=0, concat_axis=0, tiled=True)

    raw = [
        part.reshape(-1, PIECE_ROWS, PIECE)[:, SHARD:, : 2 * LANES] for part in (mine, other)
    ]
    raw = jnp.concatenate([s_shard] + raw, axis=0)
    near = neighbours(raw, "x")
    s_out = s_project(place, s_tokens.reshape(TOK, SW), (raw,) + near + opposite(near, "x"))

    out = merge(
        hr_out,
        s_out,
        cloud_valid.reshape(1, TOK),
        date_embed,
        norm_gain.reshape(1, F),
    )
    return out.reshape(DATES, ROWS, 1, F)


def solution(mesh):
    fine = Mesh(mesh.devices.reshape(4, 4, 2, 4, 4), SPACE + DATE)
    in_specs = (
        P(None, DATE, SPACE, None, None),
        P(None, DATE, SPACE, None, None),
        P(None, DATE),
        P(DATE, None),
        P(DATE),
        P(None, SPACE, DATE),
        P(),
        P(),
    )
    out_specs = P(None, SPACE, DATE, None)
    return jax.shard_map(
        per_device, mesh=fine, in_specs=in_specs, out_specs=out_specs, check_vma=False
    )
```
